256 devices in a mesh: dp: 16 (over y_lo, z), tensor: 16 (over y_hi, x, core).
Axes of the slice: x: 4, y: 4 (y_hi: 2, y_lo: 2; y = y_hi * 2 + y_lo), z: 8, core: 2. Of those that a mesh axis runs over, the one named last changes fastest.
Arguments:
- out_grad: bfloat16 [32768, 4096], P(('dp', 'tensor')), may hold values from -24 to 24
- attn_out: bfloat16 [32768, 4096], P('dp', 'tensor'), may hold values from -0.078125 to 0.078125
- o_weight: bfloat16 [4096, 4096], P('dp', 'tensor'), may hold values from -0.09375 to 0.09375
Outputs:
- attn_grad: bfloat16 [32768, 4096], P('dp', 'tensor')
- weight_grad: float32 [4096, 4096], P('dp', 'tensor')
The draws below stay inside these ranges and needn't reach their ends.
All inputs are finite; a program needn't handle non-finite values.
Results may differ from the reference program's by a relative error of at most 0.001.
Values may be sent and summed in bfloat16 or wider, within the bound.
No kernel may reach another device: no remote copies, remote signals or barrier semaphores. Data moves between devices by JAX's collectives and lax.ppermute only.
A program may use at most 64 MiB of HBM per device.

```python
import jax
import jax.numpy as jnp

D = 4096
TOK_DEV = 128
HQ = 4096
TOKENS = 32768
N_DP = 16
N_TENSOR = 16


def raised(result, rng, source, target, blocks, factor):
    def block_of(dim):
        return (jnp.arange(result.shape[dim]) // (result.shape[dim] // blocks)).reshape((-1,) + (1,) * (result.ndim - 1 - dim))

    first = jax.random.permutation(rng, blocks)[block_of(target)]
    far = (block_of(target) + blocks // 2) % blocks
    return jnp.where((block_of(source) == first) | (block_of(source) == far), factor * result, result)


def levels(rng, extent, cuts, least, top_value):
    gain, own = 1.0, jax.random.fold_in(rng, 6)
    for axis_at, shards_of in cuts:
        steps = jnp.exp(jax.random.uniform(jax.random.fold_in(own, axis_at), (shards_of,), jnp.float32, least / len(cuts), top_value / len(cuts)))
        gain = gain * jnp.repeat(steps, extent[axis_at] // shards_of).reshape([-1 if axis == axis_at else 1 for axis in range(len(extent))])
    return gain


def bell_draw(own_key, shape, spread, bound, shards=(), dtype=jnp.bfloat16):
    values = spread * jax.random.normal(own_key, shape, jnp.float32)
    if shards:
        values = values * levels(own_key, shape, shards, -0.22, 0.18)
    return jnp.clip(values, -bound, bound).astype(dtype)


def noise_with(key, dims, spread, most, split, heavy, kind=jnp.bfloat16):
    drawn = spread * jax.random.normal(key, dims, jnp.float32)
    if split:
        drawn = drawn * levels(key, dims, split, -0.22, 0.18)
    return jnp.clip(raised(drawn, jax.random.fold_in(key, 3), *heavy), -most, most).astype(kind)


def setup_inputs(seed: int = 0) -> dict:
    arg_keys = jax.random.split(jax.random.key(seed), 4)
    return {
        "out_grad": noise_with(arg_keys[0], (TOKENS, D), 1.0, 24.0, ((0, 256),), (0, 1, 256, 6.0)),
        "attn_out": bell_draw(arg_keys[1], (TOKENS, HQ), ((TOK_DEV * N_TENSOR * N_DP) ** -0.5), 0.078125, ((0, 16), (1, 16))),
        "o_weight": bell_draw(arg_keys[2], (D, HQ), HQ ** -0.5, 0.09375, ((0, 16), (1, 16))),
    }


def reference(out_grad, attn_out, o_weight):
    attn_grad = jnp.dot(out_grad, o_weight, preferred_element_type=jnp.float32).astype(jnp.bfloat16)
    weight_grad = jnp.dot(out_grad.T, attn_out, preferred_element_type=jnp.float32)
    return attn_grad, weight_grad
```

```python
import jax
import jax.numpy as jnp
import numpy as np
from jax import lax
from jax.experimental import pallas as pl
from jax.experimental.pallas import tpu as pltpu
from jax.sharding import Mesh
from jax.sharding import PartitionSpec as P

AXES = ("yl", "z", "yh", "x", "c")
SIZES = dict(yl=2, z=8, yh=2, x=4, c=2)
BF16, F32 = jnp.bfloat16, jnp.float32
HALF = 128
BLK = 256
N_Z = 8
CHUNKS = ((4, 3, 5, 2), (6, 1, 7, 0))
VMEM_LIMIT = 48 * 1024 * 1024


def permute(value, axes, target):
    shape = [SIZES[a] for a in axes]
    pairs = []
    for at in np.ndindex(*shape):
        to = target(*at)
        if to is None:
            continue
        to = tuple(v % s for v, s in zip(to, shape))
        pairs.append((int(np.ravel_multi_index(at, shape)), int(np.ravel_multi_index(to, shape))))
    return lax.ppermute(value, axes if len(axes) > 1 else axes[0], pairs)


def right(v):
    return permute(v, ("x",), lambda i: (i + 1,))


def left(v):
    return permute(v, ("x",), lambda i: (i - 1,))


def across(v):
    return permute(v, ("yh",), lambda i: (i + 1,))


def core(v):
    return permute(v, ("c",), lambda i: (i + 1,))


def z_up(v):
    return permute(v, ("z",), lambda i: (i + 1,))


def z_down(v):
    return permute(v, ("z",), lambda i: (i - 1,))


def kernel_call(kernel, out_shape, flops, nbytes, n_in, scratch=()):
    return pl.pallas_call(
        kernel,
        out_shape=out_shape,
        in_specs=[pl.BlockSpec(memory_space=pltpu.SMEM)]
        + [pl.BlockSpec(memory_space=pltpu.VMEM)] * n_in,
        out_specs=jax.tree.map(lambda _: pl.BlockSpec(memory_space=pltpu.VMEM), out_shape),
        scratch_shapes=list(scratch),
        compiler_params=pltpu.CompilerParams(vmem_limit_bytes=VMEM_LIMIT),
        cost_estimate=pl.CostEstimate(flops=flops, bytes_accessed=nbytes, transcendentals=0),
    )


def split_kernel(pos, og, *outs):
    z, c = pos[0], pos[1]
    for k, chunk in enumerate(CHUNKS):
        for who, half in ((0, 1 - c), (1, c)):
            out = outs[2 * k + who]
            for j, r in enumerate(chunk):
                col = pl.multiple_of(half * (N_Z * BLK) + lax.rem(z + r, N_Z) * BLK, BLK)
                out[:, j * BLK : (j + 1) * BLK] = og[:, pl.ds(col, BLK)]


def turn_kernel(rows, own, other, out):
    for i in range(16):
        row = pl.multiple_of(rows[i] * HALF, HALF)
        for h, src in enumerate((own, other)):
            block = src[pl.ds(row, HALF), :].astype(F32)
            out[h * BLK : (h + 1) * BLK, i * HALF : (i + 1) * HALF] = block.T.astype(BF16)


def weight_kernel(_, turned, *refs):
    pieces, outs = refs[:9], refs[9:]
    for j, out in enumerate(outs):
        rhs = jnp.concatenate([p[:, j * BLK : (j + 1) * BLK] for p in pieces], axis=0)
        out[...] = jnp.dot(turned[...], rhs, preferred_element_type=F32)


def attn_kernel(info, own_w, other_w, *refs):
    pieces = (refs[:9], refs[9:18])
    keep, send, w = refs[18:]
    z = info[16]
    for k, chunk in enumerate(CHUNKS):
        for j, r in enumerate(chunk):
            row = pl.multiple_of(lax.rem(z + r, N_Z) * BLK, BLK)
            at = (k * len(chunk) + j) * BLK
            w[at : at + BLK, :BLK] = own_w[pl.ds(row, BLK), :]
            w[at : at + BLK, BLK:] = other_w[pl.ds(row, BLK), :]
    i = 0
    for a, b in zip(*pieces):
        res = jnp.dot(
            jnp.concatenate([a[...], b[...]], axis=1), w[...], preferred_element_type=F32
        )
        for h in range(a.shape[0] // HALF):
            row = pl.multiple_of(info[i] * HALF, HALF)
            part = res[h * HALF : (h + 1) * HALF]
            keep[pl.ds(row, HALF), :] = part[:, :BLK]
            send[pl.ds(row, HALF), :] = part[:, BLK:]
            i += 1


def gather(own):
    p, l, r = across(own), right(own), left(own)
    xa = right(jnp.concatenate([l[:HALF], p[:HALF]], axis=0))
    xb = left(jnp.concatenate([r[HALF:], p[HALF:]], axis=0))
    yb = across(jnp.concatenate([l[HALF:], r[:HALF]], axis=0))
    za = right(xa[HALF:])
    zb = left(xb[HALF:])
    return [own, p, l, r, xa, xb, yb, za, zb]


def piece_rows(yh, x, c):
    def at(dy, dx, half):
        return ((yh + dy) % 2) * 8 + ((x + dx) % 4) * 2 + (c + half) % 2

    halves = [(0, 0, 0), (0, 0, 1), (1, 0, 0), (1, 0, 1), (0, -1, 0), (0, -1, 1), (0, 1, 0), (0, 1, 1)]
    halves += [(0, 2, 0), (1, -1, 0), (0, 2, 1), (1, 1, 1), (1, -1, 1), (1, 1, 0), (1, 2, 0), (1, 2, 1)]
    return [at(*h) for h in halves]


def body(out_grad, attn_out, o_weight):
    yl, z, yh, x, c = (lax.axis_index(a) for a in AXES)
    rows = piece_rows(yh, x, c)
    info = jnp.stack(rows + [z]).astype(jnp.int32)

    part = jax.ShapeDtypeStruct((HALF, 4 * BLK), BF16)
    send_a, keep_a, send_b, keep_b = kernel_call(split_kernel, (part,) * 4, 0, 2 << 20, 1)(
        jnp.stack([z, c]).astype(jnp.int32), out_grad
    )
    own_a = jnp.concatenate([keep_a, core(send_a)], axis=0)
    own_b = jnp.concatenate([keep_b, core(send_b)], axis=0)

    full_weight = lax.all_gather(o_weight, ("yl", "z"), axis=0, tiled=True)

    pieces_a = gather(own_a)
    pieces_b = gather(own_b)

    turned = kernel_call(
        turn_kernel, jax.ShapeDtypeStruct((2 * BLK, 16 * HALF), BF16), 0, 4 << 20, 2
    )(info, attn_out, core(attn_out))

    block = jax.ShapeDtypeStruct((2 * BLK, BLK), F32)
    grads = {}
    for chunk, pieces in zip(CHUNKS, (pieces_a, pieces_b)):
        made = kernel_call(
            weight_kernel, (block,) * 4, 2 * 512 * 2048 * 1024, 8 << 20, 10
        )(info, turned, *pieces)
        grads.update(zip(chunk, made))

    down = z_down(grads[4])
    up = z_up(grads[3])
    down = z_down(down + grads[5])
    up = z_up(up + grads[2])
    down = z_down(down + grads[6])
    up = z_up(up + grads[1])
    down = z_down(down + grads[7])
    total = up + grads[0] + down

    same = yl == c
    first, second = total[:BLK], total[BLK:]
    alpha = permute(
        jnp.where(same, second, first),
        ("yl", "c"),
        lambda i, j: (i, 1 - j) if i == j else (1 - i, j),
    )
    beta = permute(second, ("yl", "c"), lambda i, j: None if i == j else (1 - i, 1 - j))
    weight_grad = (alpha + jnp.where(same, first, beta)).T

    half = N_Z * BLK
    own_w = lax.dynamic_slice(full_weight, (c * half, 0), (half, BLK))
    other_w = core(lax.dynamic_slice(full_weight, ((1 - c) * half, 0), (half, BLK)))
    acc = jax.ShapeDtypeStruct((16 * HALF, BLK), F32)
    keep, send = kernel_call(
        attn_kernel,
        (acc, acc),
        2 * 2048 * 2048 * 512,
        14 << 20,
        20,
        [pltpu.VMEM((half, 2 * BLK), BF16)],
    )(info, own_w, other_w, *pieces_a, *pieces_b)
    attn_grad = (keep + core(send)).astype(BF16)
    return attn_grad, weight_grad


def solution(mesh):
    fine = Mesh(mesh.devices.reshape([SIZES[a] for a in AXES]), AXES)
    dp, tensor = ("yl", "z"), ("yh", "x", "c")
    return jax.shard_map(
        body,
        mesh=fine,
        in_specs=(P(dp + tensor, None), P(dp, tensor), P(dp, tensor)),
        out_specs=(P(dp, tensor), P(dp, tensor)),
        check_vma=False,
    )
```

```python
import functools

import jax
import jax.numpy as jnp
import numpy as np
from jax import lax
from jax.experimental import pallas as pl
from jax.experimental.pallas import tpu as pltpu
from jax.sharding import Mesh
from jax.sharding import PartitionSpec as P

AXES = ("yl", "z", "yh", "x", "c")
SIZES = dict(yl=2, z=8, yh=2, x=4, c=2)
BF16, F32 = jnp.bfloat16, jnp.float32
HALF = 128
TOK = 256
BLK = 256
FEAT = 2 * BLK
N_Z = 8
STEPS = 4
MIB = 1 << 20


def permute(value, axes, target):
    shape = [SIZES[a] for a in axes]
    pairs = []
    for at in np.ndindex(*shape):
        to = target(*at)
        if to is None:
            continue
        to = tuple(v % s for v, s in zip(to, shape))
        pairs.append((int(np.ravel_multi_index(at, shape)), int(np.ravel_multi_index(to, shape))))
    return lax.ppermute(value, axes if len(axes) > 1 else axes[0], pairs)


def along_x(v):
    return permute(v, ("x", "c"), lambda i, c: (i + 1 - 2 * c, c))


def along_z(v):
    return permute(v, ("z", "yh", "x", "c"), lambda z, y, i, c: (z - 1 + 2 * c, y, i, c))


def along_z_last(v):
    return permute(
        v, ("z", "yh", "x", "c"), lambda z, y, i, c: (z - 1, y, i, c) if c == 0 else None
    )


def against_z(v):
    return permute(v, ("z", "yh", "x", "c"), lambda z, y, i, c: (z + 1 - 2 * c, y, i, c))


def against_z_last(v):
    return permute(
        v, ("z", "yh", "x", "c"), lambda z, y, i, c: (z + 1, y, i, c) if c == 0 else None
    )


def across(v):
    return permute(v, ("yh",), lambda i: (i + 1,))


def across_other(v):
    return permute(v, ("yh", "x", "c"), lambda i, x, c: (i + 1, x, 1 - c))


def across_lo(v):
    return permute(v, ("yl",), lambda i: (i + 1,))


def core(v):
    return permute(v, ("c",), lambda i: (i + 1,))


def call(kernel, out_shape, vmem, pos, *args, scratch=(), flops=0):
    return pl.pallas_call(
        kernel,
        out_shape=out_shape,
        in_specs=[pl.BlockSpec(memory_space=pltpu.SMEM)]
        + [pl.BlockSpec(memory_space=pltpu.VMEM)] * len(args),
        out_specs=jax.tree.map(lambda _: pl.BlockSpec(memory_space=pltpu.VMEM), out_shape),
        scratch_shapes=list(scratch),
        compiler_params=pltpu.CompilerParams(vmem_limit_bytes=vmem * MIB),
        cost_estimate=pl.CostEstimate(flops=flops, bytes_accessed=1 << 16, transcendentals=0),
    )(pos, *args)


def shape(rows, columns, dtype=BF16):
    return jax.ShapeDtypeStruct((rows, columns), dtype)


def owner_row(z, core_at, step, y_lo):
    distance = jnp.where(core_at == 0, 4 + step, 3 - step)
    return pl.multiple_of((y_lo * N_Z + lax.rem(z + distance, N_Z)) * BLK, BLK)


def token_blocks(pos):
    yh, x, c = pos[1], pos[2], pos[3]
    s = 2 * c - 1

    def at(dy, dx, half):
        return lax.rem(yh + dy, 2) * 8 + lax.rem(x + dx + 4, 4) * 2 + half

    whole = ((0, 0), (1, 0), (0, s))
    out = [at(dy, dx, h) for dy, dx in whole for h in (0, 1)]
    out += [at(0, 2, c)]
    out += [at(dy, dx, h) for dy, dx in ((1, s), (1, -s), (1, 2), (0, -s)) for h in (0, 1)]
    out += [at(0, 2, 1 - c)]
    return out


def parts_of(stage):
    return [p for p in (3, 2, 1) if 0 <= stage - p < STEPS]


def offset(kind, stage, part):
    rows = {"x": {1: 2 * TOK, 2: 2 * TOK, 3: TOK}, "y": {1: TOK, 2: TOK}, "d": {2: TOK, 3: HALF}}[kind]
    at = 0
    for p in parts_of(stage):
        if p == part:
            return at
        at += rows.get(p, 0)
    return at


def pack_kernel(stage, pos, *refs):
    parts = parts_of(stage)
    z, c, yl = pos[0], pos[3], pos[4]
    refs = list(refs)
    if 1 in parts:
        mine, other = refs.pop(0), refs.pop(0)
    if stage > 1:
        x_in, y_in = refs.pop(0), refs.pop(0)
    outs = refs[-1 - (2 in parts or 1 in parts) - (2 in parts or 3 in parts) - (1 in parts) :]
    outs = list(outs)
    x_out = outs.pop(0)
    y_out = outs.pop(0) if (2 in parts or 1 in parts) else None
    d_out = outs.pop(0) if (2 in parts or 3 in parts) else None
    before = stage - 1
    if 3 in parts:
        was = offset("x", before, 2)
        to = offset("x", stage, 3)
        x_out[to : to + TOK] = x_in[was + TOK : was + 2 * TOK]
        to = offset("d", stage, 3)
        d_out[to : to + HALF] = x_in[was + HALF : was + TOK]
    if 2 in parts:
        was = offset("x", before, 1)
        to = offset("x", stage, 2)
        half = pl.multiple_of(c * HALF, HALF)
        x_out[to : to + HALF] = x_in[pl.ds(was + half, HALF), :]
        x_out[to + HALF : to + TOK] = x_in[pl.ds(was + TOK + half, HALF), :]
        had = offset("y", before, 1)
        x_out[to + TOK : to + 2 * TOK] = y_in[had : had + TOK]
        far = x_in[was + TOK : was + 2 * TOK]
        to = offset("y", stage, 2)
        y_out[to : to + TOK] = far
        to = offset("d", stage, 2)
        d_out[to : to + TOK] = far
    if 1 in parts:
        own = outs.pop(0)
        x_to, y_to = offset("x", stage, 1), offset("y", stage, 1)
        for rel in range(2):
            y_lo = lax.rem(yl + 1 + rel, 2)
            to = slice(rel * BLK, (rel + 1) * BLK)
            for which, core_at in enumerate((c, 1 - c)):
                col = owner_row(z, core_at, stage - 1, y_lo)
                for src, at in ((mine, c), (other, 1 - c)):
                    block = src[:, pl.ds(col, BLK)]
                    row = pl.multiple_of(at * HALF, HALF)
                    x_out[pl.ds(x_to + which * TOK + row, HALF), to] = block
                    if which == 0:
                        own[pl.ds(row, HALF), to] = block
                    else:
                        y_out[pl.ds(y_to + row, HALF), to] = block


def pieces_of(step, own, xs, ys, ds):
    a, b, c = step + 1, step + 2, step + 3
    x1, x2 = offset("x", a, 1), offset("x", b, 2)
    return [
        (own[step], 0, TOK),
        (ys[a], offset("y", a, 1), TOK),
        (xs[a], x1, TOK),
        (xs[b], x2, HALF),
        (xs[b], x2 + TOK, TOK),
        (ys[b], offset("y", b, 2), TOK),
        (xs[c], offset("x", c, 3), TOK),
        (ds[b], offset("d", b, 2), TOK),
        (ds[c], offset("d", c, 3), HALF),
    ]


def turn_kernel(pos, own, other, out):
    for i, block in enumerate(token_blocks(pos)):
        row = pl.multiple_of(block * HALF, HALF)
        for h, src in enumerate((own, other)):
            part = src[pl.ds(row, HALF), :].astype(F32)
            out[h * BLK : (h + 1) * BLK, i * HALF : (i + 1) * HALF] = part.T.astype(BF16)


def weight_kernel(where, _, turned, *refs):
    out = refs[-1]
    rhs = jnp.concatenate([r[at : at + n] for r, (at, n) in zip(refs, where)], axis=0)
    out[...] = jnp.dot(turned[...], rhs, preferred_element_type=F32)


def stack_kernel(_, away, own, out):
    out[:BLK] = away[...]
    out[BLK:] = own[...]


def join_kernel(_, mine, other, out):
    out[:, :BLK] = mine[...]
    out[:, BLK:] = other[...]


def attn_kernel(where, again, n_near, pos, *refs):
    near, refs = refs[:n_near], refs[n_near:]
    sums = refs[:2] if again else ()
    arrays = refs[len(sums) : -3]
    keep, send, w = refs[-3:]
    for i in range(len(where)):
        a, b = near[2 * i : 2 * i + 2]
        w[i * FEAT : (i + 1) * FEAT] = jnp.where(pos[3] == 0, a[...], b[...])
    blocks = token_blocks(pos)
    i = 0
    for p in range(9):
        n = where[0][p][2]
        lhs = jnp.concatenate(
            [arrays[step[p][0]][step[p][1] : step[p][1] + n] for step in where], axis=1
        )
        res = jnp.dot(lhs, w[...], preferred_element_type=F32)
        for h in range(n // HALF):
            rows = pl.ds(pl.multiple_of(blocks[i + h] * HALF, HALF), HALF)
            part = res[h * HALF : (h + 1) * HALF]
            for j, out in enumerate((keep, send)):
                block = part[:, j * BLK : (j + 1) * BLK]
                out[rows, :] = block + sums[j][rows, :] if again else block
        i += n // HALF


def add_kernel(_, a, b, out):
    out[...] = a[...] + b[...]


def add_split_kernel(_, a, b, out, away, own):
    total = a[...] + b[...]
    out[...] = total
    away[...] = total[:, :BLK]
    own[...] = total[:, BLK:]


def round_kernel(_, a, b, out):
    out[...] = (a[...] + b[...]).astype(BF16)


def early_kernel(_, s4, to_core, to_y):
    to_core[...] = s4[BLK:]
    to_y[...] = s4[:BLK, :BLK]


def late_kernel(_, away, early, same, cross):
    same[...] = away[:BLK] + early[:, :BLK]
    cross[...] = away[BLK:]


def cut_kernel(_, own, near):
    near[...] = own[BLK:]


def final_kernel(pos, r4, s4, early, same, cross, near, from_y, out):
    mine = pos[3] == 0

    @pl.when(mine)
    def _():
        out[...] = (r4[:BLK] + early[:, BLK:] + same[...]).T

    @pl.when(jnp.logical_not(mine))
    def _():
        out[...] = (s4[:BLK, BLK:] + from_y[...] + near[...] + cross[...]).T


def body(out_grad, attn_out, o_weight):
    yl, z, yh, x, c = (lax.axis_index(a) for a in AXES)
    pos = jnp.stack([z, yh, x, c, yl]).astype(jnp.int32)
    last = []

    def run(kernel, out_shape, vmem, *args, **more):
        args = lax.optimization_barrier((*args, *last))[: len(args)]
        out = call(kernel, out_shape, vmem, pos, *args, **more)
        last[:] = [out[-1] if isinstance(out, (tuple, list)) else out]
        return out

    def wait(*moved):
        last.extend(moved)

    def send(move, value):
        return move(lax.optimization_barrier((value, *last))[0] if last else value)

    own, xs, ys, ds = {}, {}, {}, {}

    def stage(k):
        parts = parts_of(k)
        args, outs = [], []
        if 1 in parts:
            args += [out_grad, other_grad]
        if k > 1:
            args += [xs[k - 1], ys[k - 1]] + ([ds[k - 1]] if k - 1 in ds else [])
        outs.append(shape(sum({1: 512, 2: 512, 3: 256}[p] for p in parts), FEAT))
        has_y, has_d = 2 in parts or 1 in parts, 2 in parts or 3 in parts
        if has_y:
            outs.append(shape(sum({1: 256, 2: 256, 3: 0}[p] for p in parts), FEAT))
        if has_d:
            outs.append(shape(sum({1: 0, 2: 256, 3: 128}[p] for p in parts), FEAT))
        if 1 in parts:
            outs.append(shape(TOK, FEAT))
        made = list(run(functools.partial(pack_kernel, k), tuple(outs), 8, *args))
        if 1 in parts:
            own[k - 1] = made[-1]
        xs[k] = send(along_x, made.pop(0))
        if has_y:
            ys[k] = send(across_other, made.pop(0))
        if has_d:
            ds[k] = send(core, made.pop(0))

    def weight(step):
        pieces = pieces_of(step, own, xs, ys, ds)
        kernel = functools.partial(weight_kernel, [p[1:] for p in pieces])
        return run(kernel, shape(2 * BLK, FEAT, F32), 8, turned, *[p[0] for p in pieces])

    def add(a, b):
        return run(add_kernel, shape(2 * BLK, FEAT, F32), 4, a, b)

    def attn(which, near, sums=()):
        steps = [pieces_of(s, own, xs, ys, ds) for s in which]
        near = sum(([near[4 - s], near[3 - s]] for s in which), [])
        arrays = []
        for piece in sum(steps, []):
            if all(piece[0] is not a for a in arrays):
                arrays.append(piece[0])
        where = [
            [([a is p[0] for a in arrays].index(True), p[1], p[2]) for p in step] for step in steps
        ]
        return run(
            functools.partial(attn_kernel, where, bool(sums), len(near)),
            (shape(16 * HALF, BLK, F32),) * 2, 16, *near, *sums, *arrays,
            scratch=[pltpu.VMEM((len(steps) * FEAT, 2 * BLK), BF16)],
        )

    other_grad = send(core, out_grad)
    w_away = send(across_lo, o_weight)
    other_attn = send(core, attn_out)

    stage(1)
    w_mine = run(stack_kernel, shape(FEAT, BLK), 4, w_away, o_weight)
    w_other = send(core, w_mine)
    turned = run(turn_kernel, shape(2 * BLK, 16 * HALF), 8, attn_out, other_attn)
    w0 = run(join_kernel, shape(FEAT, 2 * BLK), 4, w_mine, w_other)
    w1 = send(against_z, w0)
    wait(w1)
    stage(2)
    w2 = send(against_z, w1)
    wait(w2)
    stage(3)
    w3 = send(against_z, w2)
    wait(w3)
    stage(4)
    w4 = send(against_z_last, w3)
    g1 = weight(0)
    r1 = send(along_z, g1)
    stage(5)
    g2 = weight(1)
    s2 = add(r1, g2)
    r2 = send(along_z, s2)
    stage(6)
    g3 = weight(2)
    s3 = add(r2, g3)
    r3 = send(along_z, s3)
    near = (w0, w1, w2, w3, w4)
    sums = attn((1, 2), near)
    g4 = weight(3)
    half = shape(2 * BLK, BLK, F32)
    s4, s4_away, s4_own = run(
        add_split_kernel, (shape(2 * BLK, FEAT, F32), half, half), 4, r3, g4
    )
    r4_away, r4_own = along_z_last(s4_away), along_z_last(s4_own)
    to_core, to_y = run(early_kernel, (shape(BLK, FEAT, F32), shape(BLK, BLK, F32)), 4, s4)
    early = permute(to_core, ("c",), lambda i: (0,) if i == 1 else None)
    from_y = permute(to_y, ("yl", "c"), lambda i, j: (i + 1, j) if j == 1 else None)

    keep, out = attn((0, 3), near, sums)
    other = send(core, out)
    wait(early, from_y)
    same, cross = run(late_kernel, (shape(BLK, BLK, F32),) * 2, 4, r4_away, early)
    same = permute(same, ("yl", "c"), lambda i, j: (i + 1, 0) if j == 0 else None)
    cross = permute(cross, ("yl", "c"), lambda i, j: (i + 1, 1) if j == 0 else None)
    near = run(cut_kernel, shape(BLK, BLK, F32), 4, r4_own)
    near = permute(near, ("c",), lambda i: (1,) if i == 0 else None)
    attn_grad = run(round_kernel, shape(16 * HALF, BLK), 8, keep, other)
    weight_grad = run(
        final_kernel, shape(BLK, BLK, F32), 4, r4_own, s4, early, same, cross, near, from_y
    )
    return attn_grad, weight_grad


def solution(mesh):
    fine = Mesh(mesh.devices.reshape([SIZES[a] for a in AXES]), AXES)
    dp, tensor = ("yl", "z"), ("yh", "x", "c")
    return jax.shard_map(
        body,
        mesh=fine,
        in_specs=(P(dp + tensor, None), P(dp, tensor), P(dp, tensor)),
        out_specs=(P(dp, tensor), P(dp, tensor)),
        check_vma=False,
    )
```

```python
import functools

import jax
import jax.numpy as jnp
import numpy as np
from jax import lax
from jax.experimental import pallas as pl
from jax.experimental.pallas import tpu as pltpu
from jax.sharding import Mesh
from jax.sharding import PartitionSpec as P

AXES = ("yl", "z", "yh", "x", "c")
SIZES = dict(yl=2, z=8, yh=2, x=4, c=2)
BF16, F32 = jnp.bfloat16, jnp.float32
HALF = 128
TOK = 256
BLK = 256
FEAT = 2 * BLK
N_Z = 8
STEPS = 4
MIB = 1 << 20
SHARES = (slice(0, BLK), slice(BLK, BLK + HALF), slice(BLK + HALF, 2 * BLK))
PAD = 16


def permute(value, axes, target):
    shape = [SIZES[a] for a in axes]
    pairs = []
    for at in np.ndindex(*shape):
        to = target(*at)
        if to is None:
            continue
        to = tuple(v % s for v, s in zip(to, shape))
        pairs.append((int(np.ravel_multi_index(at, shape)), int(np.ravel_multi_index(to, shape))))
    return lax.ppermute(value, axes if len(axes) > 1 else axes[0], pairs)


def along_x(v):
    return permute(v, ("x", "c"), lambda i, c: (i + 1 - 2 * c, c))


def along_z(v):
    return permute(v, ("z", "yh", "x", "c"), lambda z, y, i, c: (z - 1 + 2 * c, y, i, c))


def along_z_last(v):
    return permute(
        v, ("z", "yh", "x", "c"), lambda z, y, i, c: (z - 1, y, i, c) if c == 0 else None
    )


def against_z(v):
    return permute(v, ("z", "yh", "x", "c"), lambda z, y, i, c: (z + 1 - 2 * c, y, i, c))


def against_z_last(v):
    return permute(
        v, ("z", "yh", "x", "c"), lambda z, y, i, c: (z + 1, y, i, c) if c == 0 else None
    )


def across(v):
    return permute(v, ("yh",), lambda i: (i + 1,))


def across_other(v):
    return permute(v, ("yh", "x", "c"), lambda i, x, c: (i + 1, x, 1 - c))


def across_lo(v):
    return permute(v, ("yl",), lambda i: (i + 1,))


def core(v):
    return permute(v, ("c",), lambda i: (i + 1,))


def call(kernel, out_shape, vmem, pos, *args, scratch=(), flops=0):
    return pl.pallas_call(
        kernel,
        out_shape=out_shape,
        in_specs=[pl.BlockSpec(memory_space=pltpu.SMEM)]
        + [pl.BlockSpec(memory_space=pltpu.VMEM)] * len(args),
        out_specs=jax.tree.map(lambda _: pl.BlockSpec(memory_space=pltpu.VMEM), out_shape),
        scratch_shapes=list(scratch),
        compiler_params=pltpu.CompilerParams(vmem_limit_bytes=vmem * MIB),
        cost_estimate=pl.CostEstimate(flops=flops, bytes_accessed=1 << 16, transcendentals=0),
    )(pos, *args)


def shape(rows, columns, dtype=BF16):
    return jax.ShapeDtypeStruct((rows, columns), dtype)


def owner_row(z, core_at, step, y_lo):
    distance = jnp.where(core_at == 0, 4 + step, 3 - step)
    return pl.multiple_of((y_lo * N_Z + lax.rem(z + distance, N_Z)) * BLK, BLK)


def token_blocks(pos):
    yh, x, c = pos[1], pos[2], pos[3]
    s = 2 * c - 1

    def at(dy, dx, half):
        return lax.rem(yh + dy, 2) * 8 + lax.rem(x + dx + 4, 4) * 2 + half

    whole = ((0, 0), (1, 0), (0, s))
    out = [at(dy, dx, h) for dy, dx in whole for h in (0, 1)]
    out += [at(0, 2, c)]
    out += [at(dy, dx, h) for dy, dx in ((1, s), (1, -s), (1, 2), (0, -s)) for h in (0, 1)]
    out += [at(0, 2, 1 - c)]
    return out


def parts_of(stage):
    return [p for p in (3, 2, 1) if 0 <= stage - p < STEPS]


def offset(kind, stage, part):
    rows = {"x": {1: 2 * TOK, 2: 2 * TOK, 3: TOK}, "y": {1: TOK, 2: TOK}, "d": {2: TOK, 3: HALF}}[kind]
    at = 0
    for p in parts_of(stage):
        if p == part:
            return at
        at += rows.get(p, 0)
    return at


def pack_kernel(stage, pos, *refs):
    parts = parts_of(stage)
    z, c, yl = pos[0], pos[3], pos[4]
    refs = list(refs)
    if 1 in parts:
        mine, other = refs.pop(0), refs.pop(0)
    if stage > 1:
        x_in, y_in = refs.pop(0), refs.pop(0)
    outs = refs[-1 - (2 in parts or 1 in parts) - (2 in parts or 3 in parts) - (1 in parts) :]
    outs = list(outs)
    x_out = outs.pop(0)
    y_out = outs.pop(0) if (2 in parts or 1 in parts) else None
    d_out = outs.pop(0) if (2 in parts or 3 in parts) else None
    before = stage - 1
    if y_out is not None:
        y_out[y_out.shape[0] - PAD :] = jnp.zeros((PAD, FEAT), BF16)
    if 3 in parts:
        was = offset("x", before, 2)
        to = offset("x", stage, 3)
        x_out[to : to + TOK] = x_in[was + TOK : was + 2 * TOK]
        to = offset("d", stage, 3)
        d_out[to : to + HALF] = x_in[was + HALF : was + TOK]
    if 2 in parts:
        was = offset("x", before, 1)
        to = offset("x", stage, 2)
        half = pl.multiple_of(c * HALF, HALF)
        x_out[to : to + HALF] = x_in[pl.ds(was + half, HALF), :]
        x_out[to + HALF : to + TOK] = x_in[pl.ds(was + TOK + half, HALF), :]
        had = offset("y", before, 1)
        x_out[to + TOK : to + 2 * TOK] = y_in[had : had + TOK]
        far = x_in[was + TOK : was + 2 * TOK]
        to = offset("y", stage, 2)
        y_out[to : to + TOK] = far
        to = offset("d", stage, 2)
        d_out[to : to + TOK] = far
    if 1 in parts:
        own = outs.pop(0)
        x_to, y_to = offset("x", stage, 1), offset("y", stage, 1)
        for rel in range(2):
            y_lo = lax.rem(yl + 1 + rel, 2)
            to = slice(rel * BLK, (rel + 1) * BLK)
            for which, core_at in enumerate((c, 1 - c)):
                col = owner_row(z, core_at, stage - 1, y_lo)
                for src, at in ((mine, c), (other, 1 - c)):
                    block = src[:, pl.ds(col, BLK)]
                    row = pl.multiple_of(at * HALF, HALF)
                    x_out[pl.ds(x_to + which * TOK + row, HALF), to] = block
                    if which == 0:
                        own[pl.ds(row, HALF), to] = block
                    else:
                        y_out[pl.ds(y_to + row, HALF), to] = block


def pieces_of(step, own, xs, ys, ds):
    a, b, c = step + 1, step + 2, step + 3
    x1, x2 = offset("x", a, 1), offset("x", b, 2)
    return [
        (own[step], 0, TOK),
        (ys[a], offset("y", a, 1), TOK),
        (xs[a], x1, TOK),
        (xs[b], x2, HALF),
        (xs[b], x2 + TOK, TOK),
        (ys[b], offset("y", b, 2), TOK),
        (xs[c], offset("x", c, 3), TOK),
        (ds[b], offset("d", b, 2), TOK),
        (ds[c], offset("d", c, 3), HALF),
    ]


def turn_kernel(pos, own, other, out):
    for i, block in enumerate(token_blocks(pos)):
        row = pl.multiple_of(block * HALF, HALF)
        for h, src in enumerate((own, other)):
            part = src[pl.ds(row, HALF), :].astype(F32)
            out[h * BLK : (h + 1) * BLK, i * HALF : (i + 1) * HALF] = part.T.astype(BF16)


def weight_kernel(where, _, turned, *refs):
    out = refs[-1]
    rhs = jnp.concatenate([r[at : at + n] for r, (at, n) in zip(refs, where)], axis=0)
    out[...] = jnp.dot(turned[...], rhs, preferred_element_type=F32)


def stack_kernel(_, away, own, out):
    out[:BLK] = away[...]
    out[BLK:] = own[...]


def join_kernel(_, mine, other, out):
    out[:, :BLK] = mine[...]
    out[:, BLK:] = other[...]


def attn_kernel(where, again, n_near, pos, *refs):
    near, refs = refs[:n_near], refs[n_near:]
    sums = refs[:3] if again else ()
    arrays = refs[len(sums) : -4]
    *outs, w = refs[-4:]
    for i in range(len(where)):
        a, b = near[2 * i : 2 * i + 2]
        w[i * FEAT : (i + 1) * FEAT] = jnp.where(pos[3] == 0, a[...], b[...])
    blocks = token_blocks(pos)
    i = 0
    for p in range(9):
        n = where[0][p][2]
        lhs = jnp.concatenate(
            [arrays[step[p][0]][step[p][1] : step[p][1] + n] for step in where], axis=1
        )
        res = jnp.dot(lhs, w[...], preferred_element_type=F32)
        for h in range(n // HALF):
            rows = pl.ds(pl.multiple_of(blocks[i + h] * HALF, HALF), HALF)
            part = res[h * HALF : (h + 1) * HALF]
            for j, (out, columns) in enumerate(zip(outs, SHARES)):
                block = part[:, columns]
                out[rows, :] = block + sums[j][rows, :] if again else block
        i += n // HALF


def add_kernel(_, a, b, out):
    out[...] = a[...] + b[...]


def round_kernel(_, keep, first, second, out):
    out[:, :HALF] = (keep[:, :HALF] + first[...]).astype(BF16)
    out[:, HALF:] = (keep[:, HALF:] + second[...]).astype(BF16)


def early_kernel(_, s4, to_core, to_y):
    to_core[...] = s4[BLK:]
    to_y[...] = s4[:BLK, :BLK]


def late_kernel(_, r4, early, same, cross, near):
    same[...] = r4[:BLK, :BLK] + early[:, :BLK]
    cross[...] = r4[BLK:, :BLK]
    near[...] = r4[BLK:, BLK:]


def final_kernel(pos, r4, s4, early, same, cross, near, from_y, out):
    mine = pos[3] == 0

    @pl.when(mine)
    def _():
        out[...] = (r4[:BLK, BLK:] + early[:, BLK:] + same[...]).T

    @pl.when(jnp.logical_not(mine))
    def _():
        out[...] = (s4[:BLK, BLK:] + from_y[...] + near[...] + cross[...]).T


def body(out_grad, attn_out, o_weight):
    yl, z, yh, x, c = (lax.axis_index(a) for a in AXES)
    pos = jnp.stack([z, yh, x, c, yl]).astype(jnp.int32)
    last = []

    def run(kernel, out_shape, vmem, *args, **more):
        args = lax.optimization_barrier((*args, *last))[: len(args)]
        out = call(kernel, out_shape, vmem, pos, *args, **more)
        last[:] = [out[-1] if isinstance(out, (tuple, list)) else out]
        return out

    def wait(*moved):
        last.extend(moved)

    def send(move, value):
        return move(lax.optimization_barrier((value, *last))[0] if last else value)

    own, xs, ys, ds = {}, {}, {}, {}

    def stage(k):
        parts = parts_of(k)
        args, outs = [], []
        if 1 in parts:
            args += [out_grad, other_grad]
        if k > 1:
            args += [xs[k - 1], ys[k - 1]] + ([ds[k - 1]] if k - 1 in ds else [])
        outs.append(shape(sum({1: 512, 2: 512, 3: 256}[p] for p in parts), FEAT))
        has_y, has_d = 2 in parts or 1 in parts, 2 in parts or 3 in parts
        if has_y:
            outs.append(shape(sum({1: 256, 2: 256, 3: 0}[p] for p in parts) + PAD, FEAT))
        if has_d:
            outs.append(shape(sum({1: 0, 2: 256, 3: 128}[p] for p in parts), FEAT))
        if 1 in parts:
            outs.append(shape(TOK, FEAT))
        made = list(run(functools.partial(pack_kernel, k), tuple(outs), 8, *args))
        if 1 in parts:
            own[k - 1] = made[-1]
        xs[k] = send(along_x, made.pop(0))
        if has_y:
            ys[k] = send(across_other, made.pop(0))
        if has_d:
            ds[k] = send(core, made.pop(0))

    def weight(step):
        pieces = pieces_of(step, own, xs, ys, ds)
        kernel = functools.partial(weight_kernel, [p[1:] for p in pieces])
        return run(kernel, shape(2 * BLK, FEAT, F32), 8, turned, *[p[0] for p in pieces])

    def add(a, b):
        return run(add_kernel, shape(2 * BLK, FEAT, F32), 4, a, b)

    def attn(which, near, sums=()):
        steps = [pieces_of(s, own, xs, ys, ds) for s in which]
        near = sum(([near[4 - s], near[3 - s]] for s in which), [])
        arrays = []
        for piece in sum(steps, []):
            if all(piece[0] is not a for a in arrays):
                arrays.append(piece[0])
        where = [
            [([a is p[0] for a in arrays].index(True), p[1], p[2]) for p in step] for step in steps
        ]
        return run(
            functools.partial(attn_kernel, where, bool(sums), len(near)),
            tuple(shape(16 * HALF, n, F32) for n in (BLK, HALF, HALF)), 16, *near, *sums, *arrays,
            scratch=[pltpu.VMEM((len(steps) * FEAT, 2 * BLK), BF16)],
        )

    other_grad = send(core, out_grad)
    w_away = send(across_lo, o_weight)
    other_attn = send(core, attn_out)

    stage(1)
    w_mine = run(stack_kernel, shape(FEAT, BLK), 4, w_away, o_weight)
    w_other = send(core, w_mine)
    w0 = run(join_kernel, shape(FEAT, 2 * BLK), 4, w_mine, w_other)
    w1 = send(against_z, w0)
    wait(w1)
    stage(2)
    turned = run(turn_kernel, shape(2 * BLK, 16 * HALF), 8, attn_out, other_attn)
    w2 = send(against_z, w1)
    wait(w2)
    stage(3)
    w3 = send(against_z, w2)
    wait(w3)
    stage(4)
    w4 = send(against_z_last, w3)
    g1 = weight(0)
    r1 = send(along_z, g1)
    stage(5)
    g2 = weight(1)
    s2 = add(r1, g2)
    r2 = send(along_z, s2)
    stage(6)
    g3 = weight(2)
    s3 = add(r2, g3)
    r3 = send(along_z, s3)
    near = (w0, w1, w2, w3, w4)
    sums = attn((1, 2), near)
    g4 = weight(3)
    s4 = add(r3, g4)
    r4 = along_z_last(s4)
    to_core, to_y = run(early_kernel, (shape(BLK, FEAT, F32), shape(BLK, BLK, F32)), 4, s4)
    early = permute(to_core, ("c",), lambda i: (0,) if i == 1 else None)
    from_y = permute(to_y, ("yl", "c"), lambda i, j: (i + 1, j) if j == 1 else None)

    keep, *out = attn((0, 3), near, sums)
    other = [send(core, o) for o in out]
    wait(early, from_y)
    same, cross, near = run(late_kernel, (shape(BLK, BLK, F32),) * 3, 4, r4, early)
    same = permute(same, ("yl", "c"), lambda i, j: (i + 1, 0) if j == 0 else None)
    cross = permute(cross, ("yl", "c"), lambda i, j: (i + 1, 1) if j == 0 else None)
    near = permute(near, ("c",), lambda i: (1,) if i == 0 else None)
    attn_grad = run(round_kernel, shape(16 * HALF, BLK), 8, keep, *other)
    weight_grad = run(
        final_kernel, shape(BLK, BLK, F32), 4, r4, s4, early, same, cross, near, from_y
    )
    return attn_grad, weight_grad


def solution(mesh):
    fine = Mesh(mesh.devices.reshape([SIZES[a] for a in AXES]), AXES)
    dp, tensor = ("yl", "z"), ("yh", "x", "c")
    return jax.shard_map(
        body,
        mesh=fine,
        in_specs=(P(dp + tensor, None), P(dp, tensor), P(dp, tensor)),
        out_specs=(P(dp, tensor), P(dp, tensor)),
        check_vma=False,
    )
```

```python
import functools

import jax
import jax.numpy as jnp
import numpy as np
from jax import lax
from jax.experimental import pallas as pl
from jax.experimental.pallas import tpu as pltpu
from jax.sharding import Mesh
from jax.sharding import PartitionSpec as P

AXES = ("yl", "z", "yh", "x", "c")
SIZES = dict(yl=2, z=8, yh=2, x=4, c=2)
BF16, F32 = jnp.bfloat16, jnp.float32
HALF = 128
TOK = 256
BLK = 256
FEAT = 2 * BLK
N_Z = 8
STEPS = 4
MIB = 1 << 20
SHARES = (slice(0, BLK), slice(BLK, BLK + HALF), slice(BLK + HALF, 2 * BLK))
PAD = 16


def permute(value, axes, target):
    shape = [SIZES[a] for a in axes]
    pairs = []
    for at in np.ndindex(*shape):
        to = target(*at)
        if to is None:
            continue
        to = tuple(v % s for v, s in zip(to, shape))
        pairs.append((int(np.ravel_multi_index(at, shape)), int(np.ravel_multi_index(to, shape))))
    return lax.ppermute(value, axes if len(axes) > 1 else axes[0], pairs)


def along_x(v):
    return permute(v, ("x", "c"), lambda i, c: (i + 1 - 2 * c, c))


def along_z(v):
    return permute(v, ("z", "yh", "x", "c"), lambda z, y, i, c: (z - 1 + 2 * c, y, i, c))


def along_z_last(v):
    return permute(
        v, ("z", "yh", "x", "c"), lambda z, y, i, c: (z - 1, y, i, c) if c == 0 else None
    )


def against_z(v):
    return permute(v, ("z", "yh", "x", "c"), lambda z, y, i, c: (z + 1 - 2 * c, y, i, c))


def against_z_last(v):
    return permute(
        v, ("z", "yh", "x", "c"), lambda z, y, i, c: (z + 1, y, i, c) if c == 0 else None
    )


def across(v):
    return permute(v, ("yh",), lambda i: (i + 1,))


def across_other(v):
    return permute(v, ("yh", "x", "c"), lambda i, x, c: (i + 1, x, 1 - c))


def across_lo(v):
    return permute(v, ("yl",), lambda i: (i + 1,))


def core(v):
    return permute(v, ("c",), lambda i: (i + 1,))


def call(kernel, out_shape, vmem, pos, *args, scratch=(), flops=0):
    return pl.pallas_call(
        kernel,
        out_shape=out_shape,
        in_specs=[pl.BlockSpec(memory_space=pltpu.SMEM)]
        + [pl.BlockSpec(memory_space=pltpu.VMEM)] * len(args),
        out_specs=jax.tree.map(lambda _: pl.BlockSpec(memory_space=pltpu.VMEM), out_shape),
        scratch_shapes=list(scratch),
        compiler_params=pltpu.CompilerParams(vmem_limit_bytes=vmem * MIB),
        cost_estimate=pl.CostEstimate(flops=flops, bytes_accessed=1 << 16, transcendentals=0),
    )(pos, *args)


def shape(rows, columns, dtype=BF16):
    return jax.ShapeDtypeStruct((rows, columns), dtype)


def owner_row(z, core_at, step, y_lo):
    distance = jnp.where(core_at == 0, 4 + step, 3 - step)
    return pl.multiple_of((y_lo * N_Z + lax.rem(z + distance, N_Z)) * BLK, BLK)


def token_blocks(pos):
    yh, x, c = pos[1], pos[2], pos[3]
    s = 2 * c - 1

    def at(dy, dx, half):
        return lax.rem(yh + dy, 2) * 8 + lax.rem(x + dx + 4, 4) * 2 + half

    whole = ((0, 0), (1, 0), (0, s))
    out = [at(dy, dx, h) for dy, dx in whole for h in (0, 1)]
    out += [at(0, 2, c)]
    out += [at(dy, dx, h) for dy, dx in ((1, s), (1, -s), (1, 2), (0, -s)) for h in (0, 1)]
    out += [at(0, 2, 1 - c)]
    return out


def parts_of(stage):
    return [p for p in (3, 2, 1) if 0 <= stage - p < STEPS]


def offset(kind, stage, part):
    rows = {"x": {1: 2 * TOK, 2: 2 * TOK, 3: TOK}, "y": {1: TOK, 2: TOK}, "d": {2: TOK, 3: HALF}}[kind]
    at = 0
    for p in parts_of(stage):
        if p == part:
            return at
        at += rows.get(p, 0)
    return at


def pack_kernel(stage, pos, *refs):
    parts = parts_of(stage)
    z, c, yl = pos[0], pos[3], pos[4]
    refs = list(refs)
    if 1 in parts:
        mine, other = refs.pop(0), refs.pop(0)
    if stage > 1:
        x_in, y_in = refs.pop(0), refs.pop(0)
    outs = refs[-1 - (2 in parts or 1 in parts) - (2 in parts or 3 in parts) - (1 in parts) :]
    outs = list(outs)
    x_out = outs.pop(0)
    y_out = outs.pop(0) if (2 in parts or 1 in parts) else None
    d_out = outs.pop(0) if (2 in parts or 3 in parts) else None
    before = stage - 1
    if y_out is not None:
        y_out[y_out.shape[0] - PAD :] = jnp.zeros((PAD, FEAT), BF16)
    if 3 in parts:
        was = offset("x", before, 2)
        to = offset("x", stage, 3)
        x_out[to : to + TOK] = x_in[was + TOK : was + 2 * TOK]
        to = offset("d", stage, 3)
        d_out[to : to + HALF] = x_in[was + HALF : was + TOK]
    if 2 in parts:
        was = offset("x", before, 1)
        to = offset("x", stage, 2)
        half = pl.multiple_of(c * HALF, HALF)
        x_out[to : to + HALF] = x_in[pl.ds(was + half, HALF), :]
        x_out[to + HALF : to + TOK] = x_in[pl.ds(was + TOK + half, HALF), :]
        had = offset("y", before, 1)
        x_out[to + TOK : to + 2 * TOK] = y_in[had : had + TOK]
        far = x_in[was + TOK : was + 2 * TOK]
        to = offset("y", stage, 2)
        y_out[to : to + TOK] = far
        to = offset("d", stage, 2)
        d_out[to : to + TOK] = far
    if 1 in parts:
        own = outs.pop(0)
        x_to, y_to = offset("x", stage, 1), offset("y", stage, 1)
        for rel in range(2):
            y_lo = lax.rem(yl + 1 + rel, 2)
            to = slice(rel * BLK, (rel + 1) * BLK)
            for which, core_at in enumerate((c, 1 - c)):
                col = owner_row(z, core_at, stage - 1, y_lo)
                for src, at in ((mine, c), (other, 1 - c)):
                    block = src[:, pl.ds(col, BLK)]
                    row = pl.multiple_of(at * HALF, HALF)
                    x_out[pl.ds(x_to + which * TOK + row, HALF), to] = block
                    if which == 0:
                        own[pl.ds(row, HALF), to] = block
                    else:
                        y_out[pl.ds(y_to + row, HALF), to] = block


def pieces_of(step, own, xs, ys, ds):
    a, b, c = step + 1, step + 2, step + 3
    x1, x2 = offset("x", a, 1), offset("x", b, 2)
    return [
        (own[step], 0, TOK),
        (ys[a], offset("y", a, 1), TOK),
        (xs[a], x1, TOK),
        (xs[b], x2, HALF),
        (xs[b], x2 + TOK, TOK),
        (ys[b], offset("y", b, 2), TOK),
        (xs[c], offset("x", c, 3), TOK),
        (ds[b], offset("d", b, 2), TOK),
        (ds[c], offset("d", c, 3), HALF),
    ]


def turn_kernel(pos, own, other, out):
    for i, block in enumerate(token_blocks(pos)):
        row = pl.multiple_of(block * HALF, HALF)
        for h, src in enumerate((own, other)):
            part = src[pl.ds(row, HALF), :].astype(F32)
            out[h * BLK : (h + 1) * BLK, i * HALF : (i + 1) * HALF] = part.T.astype(BF16)


def weight_kernel(where, _, turned, *refs):
    out = refs[-1]
    rhs = jnp.concatenate([r[at : at + n] for r, (at, n) in zip(refs, where)], axis=0)
    out[...] = jnp.dot(turned[...], rhs, preferred_element_type=F32)


def stack_kernel(_, away, own, out):
    out[:BLK] = away[...]
    out[BLK:] = own[...]


def join_kernel(_, mine, other, out):
    out[:, :BLK] = mine[...]
    out[:, BLK:] = other[...]


def attn_kernel(where, again, n_near, pos, *refs):
    near, refs = refs[:n_near], refs[n_near:]
    sums = refs[:3] if again else ()
    arrays = refs[len(sums) : -4]
    *outs, w = refs[-4:]
    for i in range(len(where)):
        a, b = near[2 * i : 2 * i + 2]
        w[i * FEAT : (i + 1) * FEAT] = jnp.where(pos[3] == 0, a[...], b[...])
    blocks = token_blocks(pos)
    i = 0
    for p in range(9):
        n = where[0][p][2]
        lhs = jnp.concatenate(
            [arrays[step[p][0]][step[p][1] : step[p][1] + n] for step in where], axis=1
        )
        res = jnp.dot(lhs, w[...], preferred_element_type=F32)
        for h in range(n // HALF):
            rows = pl.ds(pl.multiple_of(blocks[i + h] * HALF, HALF), HALF)
            part = res[h * HALF : (h + 1) * HALF]
            for j, (out, columns) in enumerate(zip(outs, SHARES)):
                block = part[:, columns]
                out[rows, :] = block + sums[j][rows, :] if again else block
        i += n // HALF


def add_kernel(_, a, b, out):
    out[...] = a[...] + b[...]


def round_kernel(_, keep, first, second, out):
    out[:, :HALF] = (keep[:, :HALF] + first[...]).astype(BF16)
    out[:, HALF:] = (keep[:, HALF:] + second[...]).astype(BF16)


def early_kernel(_, s4, to_core, to_y):
    to_core[...] = s4[BLK:]
    to_y[...] = s4[:BLK, :BLK]


def late_kernel(_, r4, early, same, cross, near):
    same[...] = r4[:BLK, :BLK] + early[:, :BLK]
    cross[...] = r4[BLK:, :BLK]
    near[...] = r4[BLK:, BLK:]


def final_kernel(pos, r4, s4, early, same, cross, near, from_y, out):
    mine = pos[3] == 0

    @pl.when(mine)
    def _():
        out[...] = (r4[:BLK, BLK:] + early[:, BLK:] + same[...]).T

    @pl.when(jnp.logical_not(mine))
    def _():
        out[...] = (s4[:BLK, BLK:] + from_y[...] + near[...] + cross[...]).T


def body(out_grad, attn_out, o_weight):
    yl, z, yh, x, c = (lax.axis_index(a) for a in AXES)
    pos = jnp.stack([z, yh, x, c, yl]).astype(jnp.int32)
    last = []

    def run(kernel, out_shape, vmem, *args, **more):
        args = lax.optimization_barrier((*args, *last))[: len(args)]
        out = call(kernel, out_shape, vmem, pos, *args, **more)
        last[:] = [out[-1] if isinstance(out, (tuple, list)) else out]
        return out

    def wait(*moved):
        last.extend(moved)

    def send(move, value):
        return move(lax.optimization_barrier((value, *last))[0] if last else value)

    own, xs, ys, ds = {}, {}, {}, {}

    def stage(k):
        parts = parts_of(k)
        args, outs = [], []
        if 1 in parts:
            args += [out_grad, other_grad]
        if k > 1:
            args += [xs[k - 1], ys[k - 1]] + ([ds[k - 1]] if k - 1 in ds else [])
        outs.append(shape(sum({1: 512, 2: 512, 3: 256}[p] for p in parts), FEAT))
        has_y, has_d = 2 in parts or 1 in parts, 2 in parts or 3 in parts
        if has_y:
            outs.append(shape(sum({1: 256, 2: 256, 3: 0}[p] for p in parts) + PAD, FEAT))
        if has_d:
            outs.append(shape(sum({1: 0, 2: 256, 3: 128}[p] for p in parts), FEAT))
        if 1 in parts:
            outs.append(shape(TOK, FEAT))
        made = list(run(functools.partial(pack_kernel, k), tuple(outs), 8, *args))
        if 1 in parts:
            own[k - 1] = made[-1]
        xs[k] = send(along_x, made.pop(0))
        if has_y:
            ys[k] = send(across_other, made.pop(0))
        if has_d:
            ds[k] = send(core, made.pop(0))

    def weight(step):
        pieces = pieces_of(step, own, xs, ys, ds)
        kernel = functools.partial(weight_kernel, [p[1:] for p in pieces])
        return run(kernel, shape(2 * BLK, FEAT, F32), 8, turned, *[p[0] for p in pieces])

    def add(a, b):
        return run(add_kernel, shape(2 * BLK, FEAT, F32), 4, a, b)

    def attn(which, near, sums=()):
        steps = [pieces_of(s, own, xs, ys, ds) for s in which]
        near = sum(([near[4 - s], near[3 - s]] for s in which), [])
        arrays = []
        for piece in sum(steps, []):
            if all(piece[0] is not a for a in arrays):
                arrays.append(piece[0])
        where = [
            [([a is p[0] for a in arrays].index(True), p[1], p[2]) for p in step] for step in steps
        ]
        return run(
            functools.partial(attn_kernel, where, bool(sums), len(near)),
            tuple(shape(16 * HALF, n, F32) for n in (BLK, HALF, HALF)), 16, *near, *sums, *arrays,
            scratch=[pltpu.VMEM((len(steps) * FEAT, 2 * BLK), BF16)],
        )

    other_grad = send(core, out_grad)
    w_away = send(across_lo, o_weight)
    other_attn = send(core, attn_out)

    stage(1)
    w_mine = run(stack_kernel, shape(FEAT, BLK), 4, w_away, o_weight)
    w_other = send(core, w_mine)
    w0 = run(join_kernel, shape(FEAT, 2 * BLK), 4, w_mine, w_other)
    w1 = send(against_z, w0)
    wait(w1)
    stage(2)
    turned = run(turn_kernel, shape(2 * BLK, 16 * HALF), 8, attn_out, other_attn)
    w2 = send(against_z, w1)
    wait(w2)
    stage(3)
    w3 = send(against_z, w2)
    wait(w3)
    stage(4)
    w4 = send(against_z_last, w3)
    g1 = weight(0)
    r1 = send(along_z, g1)
    stage(5)
    g2 = weight(1)
    s2 = add(r1, g2)
    r2 = send(along_z, s2)
    g3 = weight(2)
    s3 = add(r2, g3)
    r3 = send(along_z, s3)
    stage(6)
    near = (w0, w1, w2, w3, w4)
    sums = attn((1, 2), near)
    g4 = weight(3)
    s4 = add(r3, g4)
    r4 = along_z_last(s4)
    to_core, to_y = run(early_kernel, (shape(BLK, FEAT, F32), shape(BLK, BLK, F32)), 4, s4)
    early = permute(to_core, ("c",), lambda i: (0,) if i == 1 else None)
    from_y = permute(to_y, ("yl", "c"), lambda i, j: (i + 1, j) if j == 1 else None)

    keep, *out = attn((0, 3), near, sums)
    other = [send(core, o) for o in out]
    wait(early, from_y)
    same, cross, near = run(late_kernel, (shape(BLK, BLK, F32),) * 3, 4, r4, early)
    same = permute(same, ("yl", "c"), lambda i, j: (i + 1, 0) if j == 0 else None)
    cross = permute(cross, ("yl", "c"), lambda i, j: (i + 1, 1) if j == 0 else None)
    near = permute(near, ("c",), lambda i: (1,) if i == 0 else None)
    attn_grad = run(round_kernel, shape(16 * HALF, BLK), 8, keep, *other)
    weight_grad = run(
        final_kernel, shape(BLK, BLK, F32), 4, r4, s4, early, same, cross, near, from_y
    )
    return attn_grad, weight_grad


def solution(mesh):
    fine = Mesh(mesh.devices.reshape([SIZES[a] for a in AXES]), AXES)
    dp, tensor = ("yl", "z"), ("yh", "x", "c")
    return jax.shard_map(
        body,
        mesh=fine,
        in_specs=(P(dp + tensor, None), P(dp, tensor), P(dp, tensor)),
        out_specs=(P(dp, tensor), P(dp, tensor)),
        check_vma=False,
    )
```
